32 devices in a mesh: req: 4 (over x, core), kv: 8 (over z, y).
Axes of the slice: x: 2, y: 2, z: 4, core: 2. Of those that a mesh axis runs over, the one named last changes fastest.
Arguments:
- hidden_in: bfloat16 [2048, 4096], P('req'), may hold values from -6 to 6
- ln_gains: float32 [2, 4096], replicated, may hold values from 0.1 to 1.9
- qkv_weight: bfloat16 [4096, 3, 4096], P('req', None, 'kv'), may hold values from -0.09375 to 0.09375
- dense_weight: bfloat16 [4096, 4096], P('kv', 'req'), may hold values from -0.09375 to 0.09375
- up_weight: bfloat16 [4096, 16384], P('req', 'kv'), may hold values from -0.09375 to 0.09375
- down_weight: bfloat16 [16384, 4096], P('kv', 'req'), may hold values from -0.046875 to 0.046875
- cache: bfloat16 [4, 64, 2, 32, 128, 128], P('req', 'kv'), may hold values from -200 to 200
- cached_len: int32 [8], P('req'), may hold values from 1 to 4096, as said below
- page_table: int32 [8, 32], P('req'), may hold values from 0 to 63, as said below
Outputs:
- hidden_out: float32 [2048, 4096], P('req', 'kv')
The draws below stay inside these ranges and needn't reach their ends.
Inputs may be any that keep to these rules, and one draw needn't show every extreme that they name: `page_table`: within each group of 2 consecutive requests the entries are distinct and together name each of the group's 64 slots once. `cached_len`: some request has exactly 4096 cached tokens.
All inputs are finite; a program needn't handle non-finite values.
Results may differ from the reference program's by a relative error of at most 0.012.
The reference program's roundings to bfloat16 on the way count: a program that leaves them out, or rounds other values in their place, can miss the bound.
Values may be sent and summed in bfloat16 or wider, within the bound.
A program may use at most 192 MiB of HBM per device.

```python
import jax
import jax.numpy as jnp
from jax import lax

D = 4096
HEADS = 32
HD = 128
ROT = 32
FF = 16384
REQ_GRP = 2
SPAN = 256
PAGE = 128
GROUPS = 4
REQS = 8
SLOTS = 64
MAXP = 32
MAXLEN = 4096
TOKENS = 2048


def draw_cache(key, part):
    values = jax.random.normal(key, (GROUPS, SLOTS, 2, HEADS, PAGE, HD), jnp.float32)
    return jnp.clip(values, -200.0, 200.0).astype(jnp.bfloat16)


def draw_cached_len(key, part):
    base = jax.random.randint(key, (REQS,), 1, MAXLEN + 1, jnp.int32)
    pick = jax.random.randint(jax.random.fold_in(key, 1), (), 0, REQS, jnp.int32)
    return base.at[pick].set(MAXLEN)


def draw_page_table(key, part):
    keys = jax.random.split(key, GROUPS)
    perms = jax.vmap(lambda k: jax.random.permutation(k, SLOTS))(keys)
    return perms.reshape(REQS, MAXP).astype(jnp.int32)


def block_levels(key, extent, pieces, low, top_value):
    level = 1.0
    for dim, parts in pieces:
        heights = jax.random.uniform(jax.random.fold_in(jax.random.fold_in(key, 6), dim), (parts,), jnp.float32, low / len(pieces), top_value / len(pieces))
        level = level * jnp.repeat(jnp.exp(heights), extent[dim] // parts).reshape((-1,) + (1,) * (len(extent) - 1 - dim))
    return level


def bell_draw(key, shape, scale, reach, shards=(), held_as=jnp.bfloat16):
    factor_of = block_levels(key, shape, shards, -0.22, 0.18) if shards else 1.0
    array = jax.random.normal(key, shape, jnp.float32) * scale * factor_of
    return jnp.minimum(jnp.maximum(array, -reach), reach).astype(held_as)


def setup_inputs(seed: int = 0) -> dict:
    arg_keys = jax.random.split(jax.random.key(seed), 10)
    hidden_in = bell_draw(arg_keys[0], (TOKENS, D), 1.0, 6.0, ((0, 4),))
    ln_gains = jnp.clip(1.0 + 0.18 * jax.random.normal(arg_keys[1], (2, D), jnp.float32), 0.1, 1.9)
    qkv_weight = bell_draw(arg_keys[2], (D, 3, D), D ** -0.5, 0.09375, ((0, 4), (2, 8)))
    dense_weight = bell_draw(arg_keys[3], (D, D), D ** -0.5, 0.09375, ((0, 8), (1, 4)))
    up_weight = bell_draw(arg_keys[4], (D, FF), D ** -0.5, 0.09375, ((0, 4), (1, 8)))
    down_weight = bell_draw(arg_keys[5], (FF, D), FF ** -0.5, 0.046875, ((0, 8), (1, 4)))
    cache = draw_cache(jax.random.fold_in(arg_keys[9], 71), 0)
    cached_len = draw_cached_len(jax.random.fold_in(arg_keys[9], 71), 0)
    page_table = draw_page_table(jax.random.fold_in(arg_keys[9], 71), 0)
    return {"hidden_in": hidden_in, "ln_gains": ln_gains, "qkv_weight": qkv_weight, "dense_weight": dense_weight, "up_weight": up_weight, "down_weight": down_weight, "cache": cache, "cached_len": cached_len, "page_table": page_table}


def layer_norm(x, gain):
    mean = lax.optimization_barrier(jnp.mean(x, axis=-1, keepdims=True))
    cent = x - mean
    var = lax.optimization_barrier(jnp.mean(cent * cent, axis=-1, keepdims=True))
    return cent * jax.lax.rsqrt(var + 1e-05) * gain

def rotate(t, pos):
    half = ROT // 2
    freq = 10000.0 ** (-(jnp.arange(half, dtype=jnp.float32) * 2.0 / ROT))
    angle = pos[:, None] * freq[None, :]
    cosine = jnp.cos(angle)[:, None, :]
    sine = jnp.sin(angle)[:, None, :]
    first = t[..., :half]
    second = t[..., half:ROT]
    return jnp.concatenate([first * cosine - second * sine, second * cosine + first * sine, t[..., ROT:]], axis=-1)

def reference(hidden_in, ln_gains, qkv_weight, dense_weight, up_weight, down_weight, cache, cached_len, page_table):
    x = hidden_in.astype(jnp.float32)
    h1 = layer_norm(x, ln_gains[0]).astype(jnp.bfloat16)
    h2 = layer_norm(x, ln_gains[1]).astype(jnp.bfloat16)
    qkv = jnp.dot(h1, qkv_weight.reshape(D, 3 * D), preferred_element_type=jnp.float32).reshape(TOKENS, 3, HEADS, HD)
    offsets = jnp.arange(SPAN, dtype=jnp.int32)
    pos = (cached_len[:, None] + offsets[None, :]).reshape(TOKENS).astype(jnp.float32)
    query = rotate(qkv[:, 0], pos).astype(jnp.bfloat16)
    key = rotate(qkv[:, 1], pos).astype(jnp.bfloat16)
    value = qkv[:, 2].astype(jnp.bfloat16)
    scale = 1.0 / HD ** 0.5
    causal = offsets[None, :] <= offsets[:, None]
    outputs = []
    for req in range(REQS):
        group = req // REQ_GRP
        q_req = query[req * SPAN:(req + 1) * SPAN].astype(jnp.float32)
        k_req = key[req * SPAN:(req + 1) * SPAN].astype(jnp.float32)
        v_req = value[req * SPAN:(req + 1) * SPAN].astype(jnp.float32)
        pages = cache[group][page_table[req]]
        k_old = jnp.transpose(pages[:, 0], (1, 0, 2, 3)).reshape(HEADS, MAXLEN, HD).astype(jnp.float32)
        v_old = jnp.transpose(pages[:, 1], (1, 0, 2, 3)).reshape(HEADS, MAXLEN, HD).astype(jnp.float32)
        live = jnp.arange(MAXLEN, dtype=jnp.int32) < cached_len[req]
        s_old = jnp.einsum('qhd,hkd->hqk', q_req, k_old) * scale
        s_new = jnp.einsum('qhd,khd->hqk', q_req, k_req) * scale
        s_old = jnp.where(live[None, None, :], s_old, -1e+30)
        s_new = jnp.where(causal[None], s_new, -1e+30)
        top = jnp.maximum(lax.optimization_barrier(jnp.max(s_old, axis=-1)), lax.optimization_barrier(jnp.max(s_new, axis=-1)))
        p_old = jnp.where(live[None, None, :], jnp.exp(s_old - top[..., None]), 0.0).astype(jnp.bfloat16).astype(jnp.float32)
        p_new = jnp.where(causal[None], jnp.exp(s_new - top[..., None]), 0.0).astype(jnp.bfloat16).astype(jnp.float32)
        numer = jnp.einsum('hqk,hkd->hqd', p_old, v_old) + jnp.einsum('hqk,khd->hqd', p_new, v_req)
        denom = lax.optimization_barrier(jnp.sum(p_old, axis=-1)) + lax.optimization_barrier(jnp.sum(p_new, axis=-1))
        att = numer / denom[..., None]
        outputs.append(jnp.transpose(att, (1, 0, 2)).reshape(SPAN, D))
    attn = jnp.concatenate(outputs, axis=0).astype(jnp.bfloat16)
    branch = jnp.dot(attn, dense_weight, preferred_element_type=jnp.float32)
    hidden = jax.nn.gelu(jnp.dot(h2, up_weight, preferred_element_type=jnp.float32), approximate=False).astype(jnp.bfloat16)
    mlp = jnp.dot(hidden, down_weight, preferred_element_type=jnp.float32)
    return x + branch + mlp
```

```python
import functools

import jax
import jax.numpy as jnp
from jax import lax
from jax.experimental import pallas as pl
from jax.experimental.pallas import tpu as pltpu
from jax.sharding import PartitionSpec as P

D = 4096
HEADS = 32
HD = 128
ROT = 32
PAGE = 128
LOW = -1e30
FLOOR = -1e29


def layer_norm(x, gain):
    mean = jnp.mean(x, axis=-1, keepdims=True)
    cent = x - mean
    var = jnp.mean(cent * cent, axis=-1, keepdims=True)
    return cent * lax.rsqrt(var + 1e-05) * gain


def rotate(t, pos):
    half = ROT // 2
    freq = 10000.0 ** (-(jnp.arange(half, dtype=jnp.float32) * 2.0 / ROT))
    angle = pos[:, None] * freq[None, :]
    cosine = jnp.cos(angle)[:, None, :]
    sine = jnp.sin(angle)[:, None, :]
    first = t[..., :half]
    second = t[..., half:ROT]
    return jnp.concatenate(
        [first * cosine - second * sine, second * cosine + first * sine, t[..., ROT:]], axis=-1
    )


def exchange_kernel(n, views, n_arrays, *refs):
    srcs = refs[:n_arrays]
    dsts = refs[n_arrays : 2 * n_arrays]
    send_sem, recv_sem, local_sem = refs[2 * n_arrays :]
    me = lax.axis_index("kv")

    barrier = pltpu.get_barrier_semaphore()
    for off in range(1, n):
        pl.semaphore_signal(
            barrier,
            inc=1,
            device_id={"kv": lax.rem(me + off, n)},
            device_id_type=pl.DeviceIdType.MESH,
        )
    pl.semaphore_wait(barrier, n - 1)

    copies = []
    for off in range(n - 1, 0, -1):
        peer = lax.rem(me + off, n)
        for i in range(n_arrays):
            copy = pltpu.make_async_remote_copy(
                src_ref=views[i](srcs[i], peer),
                dst_ref=dsts[i].at[me],
                send_sem=send_sem.at[i, off],
                recv_sem=recv_sem.at[i, off],
                device_id={"kv": peer},
                device_id_type=pl.DeviceIdType.MESH,
            )
            copy.start()
            copies.append(copy)
    for i in range(n_arrays):
        own = pltpu.make_async_copy(views[i](srcs[i], me), dsts[i].at[me], local_sem.at[i])
        own.start()
        copies.append(own)
    for copy in copies:
        copy.wait()


def exchange(arrays, views, shapes, n, collective_id, cost_us):
    count = len(arrays)
    return pl.pallas_call(
        functools.partial(exchange_kernel, n, views, count),
        out_shape=[
            jax.ShapeDtypeStruct((n,) + shape, a.dtype) for shape, a in zip(shapes, arrays)
        ],
        in_specs=[pl.BlockSpec(memory_space=pl.ANY)] * count,
        out_specs=[pl.BlockSpec(memory_space=pl.ANY)] * count,
        scratch_shapes=[
            pltpu.SemaphoreType.DMA((count, n)),
            pltpu.SemaphoreType.DMA((count, n)),
            pltpu.SemaphoreType.DMA((count,)),
        ],
        compiler_params=pltpu.CompilerParams(collective_id=collective_id, has_side_effects=True),
        cost_estimate=pl.CostEstimate(
            flops=0, bytes_accessed=int(cost_us * 3.0e6), transcendentals=0
        ),
    )(*arrays)


def attention_kernel(
    groups, span, heads, slots, owner_ref, base_ref, len_ref, q_ref, cache_ref, acc_ref, stat_ref,
    s_scr, a_scr,
):
    scale = 1.0 / HD**0.5
    place = lax.broadcasted_iota(jnp.int32, (PAGE, span), 0)
    half = stat_ref.shape[2] // 2
    stat_ref[...] = jnp.zeros_like(stat_ref)
    for h in range(heads):
        tops = [jnp.full((1, span), FLOOR, jnp.float32) for _ in range(groups)]
        for s in range(slots):
            owner = owner_ref[s]
            q = q_ref[0, pl.ds(pl.multiple_of(owner * span, span), span), h * HD : (h + 1) * HD]
            st = lax.dot_general(
                cache_ref[s, 0, h], q, (((1,), (1,)), ((), ())), preferred_element_type=jnp.float32
            )
            st = jnp.where(place < len_ref[owner] - base_ref[s], st * scale, LOW)
            s_scr[s] = st
            col = jnp.max(st, axis=0, keepdims=True)
            tops = [jnp.maximum(t, jnp.where(owner == r, col, LOW)) for r, t in enumerate(tops)]
        sums = [jnp.zeros((1, span), jnp.float32) for _ in range(groups)]
        a_scr[...] = jnp.zeros_like(a_scr)
        for s in range(slots):
            owner = owner_ref[s]
            top = tops[0]
            for r in range(1, groups):
                top = jnp.where(owner == r, tops[r], top)
            p = jnp.exp(s_scr[s] - top).astype(jnp.bfloat16)
            part = jnp.sum(p.astype(jnp.float32), axis=0, keepdims=True)
            sums = [t + jnp.where(owner == r, part, 0.0) for r, t in enumerate(sums)]
            a_scr[owner] += lax.dot_general(
                cache_ref[s, 1, h], p, (((0,), (0,)), ((), ())), preferred_element_type=jnp.float32
            )
        for r in range(groups):
            acc_ref[0, r, h] = a_scr[r].astype(jnp.bfloat16)
            stat_ref[0, r, h : h + 1, :] = tops[r]
            stat_ref[0, r, half + h : half + h + 1, :] = sums[r]


def paged_attention(q_all, local_cache, owner_req, base, cached_len, groups, span, heads, half):
    n = q_all.shape[0]
    slots = local_cache.shape[0]
    rows, width = q_all.shape[1:]
    smem = pl.BlockSpec(memory_space=pltpu.SMEM)
    return pl.pallas_call(
        functools.partial(attention_kernel, groups, span, heads, slots),
        grid=(n,),
        out_shape=[
            jax.ShapeDtypeStruct((n, groups, heads, HD, span), jnp.bfloat16),
            jax.ShapeDtypeStruct((n, groups, 2 * half, span), jnp.float32),
        ],
        in_specs=[
            smem,
            smem,
            smem,
            pl.BlockSpec((1, rows, width), lambda j: (j, 0, 0)),
            pl.BlockSpec((slots, 2, heads, PAGE, HD), lambda j: (0, 0, j, 0, 0)),
        ],
        out_specs=[
            pl.BlockSpec((1, groups, heads, HD, span), lambda j: (j, 0, 0, 0, 0)),
            pl.BlockSpec((1, groups, 2 * half, span), lambda j: (j, 0, 0, 0)),
        ],
        scratch_shapes=[
            pltpu.VMEM((slots, PAGE, span), jnp.float32),
            pltpu.VMEM((groups, HD, span), jnp.float32),
        ],
        compiler_params=pltpu.CompilerParams(vmem_limit_bytes=32 * 1024 * 1024),
        cost_estimate=pl.CostEstimate(
            flops=4 * slots * HEADS * span * PAGE * HD,
            bytes_accessed=60_000_000,
            transcendentals=slots * HEADS * span * PAGE,
        ),
    )(owner_req, base, cached_len, q_all, local_cache)


def after(x, y):
    return lax.optimization_barrier((x, y))[0]


def per_device(
    hidden_in,
    ln_gains,
    qkv_weight,
    dense_weight,
    up_weight,
    down_weight,
    cache,
    cached_len,
    page_table,
):
    n_kv = lax.axis_size("kv")
    me_kv = lax.axis_index("kv")
    rows = hidden_in.shape[0]
    groups_here = cached_len.shape[0]
    span_rows = rows // groups_here
    width_loc = qkv_weight.shape[2]
    heads_loc = width_loc // HD
    half = max(4, heads_loc)
    scale = 1.0 / HD**0.5
    x = hidden_in.astype(jnp.float32)
    h1 = layer_norm(x, ln_gains[0]).astype(jnp.bfloat16)
    h2 = layer_norm(x, ln_gains[1]).astype(jnp.bfloat16)
    qkv_piece = lax.all_gather(qkv_weight, "req", axis=0, tiled=True)
    up_piece = lax.all_gather(after(up_weight, qkv_piece), "req", axis=0, tiled=True)
    dense_piece = lax.all_gather(after(dense_weight, up_piece), "req", axis=1, tiled=True)
    down_piece = lax.all_gather(after(down_weight, dense_piece), "req", axis=1, tiled=True)
    count = qkv_piece.shape[0]
    qkv = jnp.dot(
        h1, qkv_piece.reshape(count, 3 * width_loc), preferred_element_type=jnp.float32
    )
    qkv = qkv.reshape(rows, 3, heads_loc, HD)
    offsets = jnp.arange(span_rows, dtype=jnp.int32)
    pos = (cached_len[:, None] + offsets[None, :]).reshape(rows).astype(jnp.float32)
    query = rotate(qkv[:, 0], pos).astype(jnp.bfloat16)
    key_new = rotate(qkv[:, 1], pos).astype(jnp.bfloat16)
    value_new = qkv[:, 2].astype(jnp.bfloat16)

    whole = lambda ref, peer: ref
    block = lambda ref, peer: ref.at[peer]
    (q_all,) = exchange(
        [query.reshape(rows, width_loc)], [whole], [(rows, width_loc)], n_kv, 1, 80
    )

    local_cache = cache[0]
    slots_here = local_cache.shape[0]
    slot_ids = me_kv * slots_here + jnp.arange(slots_here, dtype=jnp.int32)
    match = (page_table[None, :, :] == slot_ids[:, None, None]).astype(jnp.int32)
    owner_req = jnp.sum(
        match * jnp.arange(groups_here, dtype=jnp.int32)[None, :, None], axis=(1, 2)
    )
    owner_page = jnp.sum(
        match * jnp.arange(page_table.shape[1], dtype=jnp.int32)[None, None, :], axis=(1, 2)
    )
    acc, stat = paged_attention(
        q_all,
        local_cache,
        owner_req,
        owner_page * PAGE,
        cached_len,
        groups_here,
        span_rows,
        heads_loc,
        half,
    )
    acc_in, stat_in = exchange(
        [acc, stat], [block, block], [acc.shape[1:], stat.shape[1:]], n_kv, 2, 80
    )

    q_grp = query.reshape(groups_here, span_rows, heads_loc, HD)
    k_grp = key_new.reshape(groups_here, span_rows, heads_loc, HD)
    v_grp = value_new.reshape(groups_here, span_rows, heads_loc, HD)
    causal = (offsets[None, :] <= offsets[:, None])[None, None]
    s_new = jnp.einsum("gqhd,gkhd->ghqk", q_grp, k_grp, preferred_element_type=jnp.float32) * scale
    s_new = jnp.where(causal, s_new, LOW)
    top_new = jnp.max(s_new, axis=-1)
    p_new = jnp.where(causal, jnp.exp(s_new - top_new[..., None]), 0.0).astype(jnp.bfloat16)
    total_new = jnp.sum(p_new.astype(jnp.float32), axis=-1)
    accum_new = jnp.einsum("ghqk,gkhd->ghdq", p_new, v_grp, preferred_element_type=jnp.float32)

    tops = stat_in[:, :, :heads_loc, :]
    totals = stat_in[:, :, half : half + heads_loc, :]
    largest = jnp.maximum(jnp.max(tops, axis=0), top_new)
    factor = jnp.exp(tops - largest[None])
    fresh = jnp.exp(top_new - largest)
    denom = jnp.sum(totals * factor, axis=0) + total_new * fresh
    numer = jnp.sum(acc_in.astype(jnp.float32) * factor[:, :, :, None, :], axis=0)
    numer = numer + accum_new * fresh[:, :, None, :]
    att = (numer / denom[:, :, None, :]).astype(jnp.bfloat16)
    att = jnp.transpose(att, (0, 3, 1, 2)).reshape(rows, width_loc)

    up_acc = jnp.dot(h2, up_piece, preferred_element_type=jnp.float32)
    hidden = jax.nn.gelu(up_acc, approximate=False).astype(jnp.bfloat16)
    value = jnp.dot(att, dense_piece, preferred_element_type=jnp.float32) + jnp.dot(
        hidden, down_piece, preferred_element_type=jnp.float32
    )
    width_out = D // n_kv
    strip = lambda ref, peer: ref.at[
        :, pl.ds(pl.multiple_of(peer * width_out, width_out), width_out)
    ]
    (parts,) = exchange(
        [value.astype(jnp.bfloat16)], [strip], [(rows, width_out)], n_kv, 3, 80
    )
    residual = lax.dynamic_slice_in_dim(hidden_in, me_kv * width_out, width_out, 1)
    return residual.astype(jnp.float32) + jnp.sum(parts.astype(jnp.float32), axis=0)


def solution(mesh):
    placed = (
        P("req", None),
        P(),
        P("req", None, "kv"),
        P("kv", "req"),
        P("req", "kv"),
        P("kv", "req"),
        P("req", "kv", None, None, None, None),
        P("req"),
        P("req", None),
    )
    return jax.shard_map(
        per_device, mesh=mesh, in_specs=placed, out_specs=P("req", "kv"), check_vma=False
    )
```

```python
import functools

import jax
import jax.numpy as jnp
from jax import lax
from jax.experimental import pallas as pl
from jax.experimental.pallas import tpu as pltpu
from jax.sharding import PartitionSpec as P

D = 4096
HEADS = 32
HD = 128
ROT = 32
PAGE = 128
LOW = -1e30
FLOOR = -1e29


def layer_norm(x, gain):
    mean = jnp.mean(x, axis=-1, keepdims=True)
    cent = x - mean
    var = jnp.mean(cent * cent, axis=-1, keepdims=True)
    return cent * lax.rsqrt(var + 1e-05) * gain


def rotate(t, pos):
    half = ROT // 2
    freq = 10000.0 ** (-(jnp.arange(half, dtype=jnp.float32) * 2.0 / ROT))
    angle = pos[:, None] * freq[None, :]
    cosine = jnp.cos(angle)[:, None, :]
    sine = jnp.sin(angle)[:, None, :]
    first = t[..., :half]
    second = t[..., half:ROT]
    return jnp.concatenate(
        [first * cosine - second * sine, second * cosine + first * sine, t[..., ROT:]], axis=-1
    )


def exchange_kernel(n, views, n_arrays, *refs):
    srcs = refs[:n_arrays]
    dsts = refs[n_arrays : 2 * n_arrays]
    send_sem, recv_sem, local_sem = refs[2 * n_arrays :]
    me = lax.axis_index("kv")

    barrier = pltpu.get_barrier_semaphore()
    for off in range(1, n):
        pl.semaphore_signal(
            barrier,
            inc=1,
            device_id={"kv": lax.rem(me + off, n)},
            device_id_type=pl.DeviceIdType.MESH,
        )
    pl.semaphore_wait(barrier, n - 1)

    copies = []
    for off in range(n - 1, 0, -1):
        peer = lax.rem(me + off, n)
        for i in range(n_arrays):
            copy = pltpu.make_async_remote_copy(
                src_ref=views[i](srcs[i], peer),
                dst_ref=dsts[i].at[me],
                send_sem=send_sem.at[i, off],
                recv_sem=recv_sem.at[i, off],
                device_id={"kv": peer},
                device_id_type=pl.DeviceIdType.MESH,
            )
            copy.start()
            copies.append(copy)
    for i in range(n_arrays):
        own = pltpu.make_async_copy(views[i](srcs[i], me), dsts[i].at[me], local_sem.at[i])
        own.start()
        copies.append(own)
    for copy in copies:
        copy.wait()


def exchange(arrays, views, shapes, n, collective_id, cost_us):
    count = len(arrays)
    return pl.pallas_call(
        functools.partial(exchange_kernel, n, views, count),
        out_shape=[
            jax.ShapeDtypeStruct((n,) + shape, a.dtype) for shape, a in zip(shapes, arrays)
        ],
        in_specs=[pl.BlockSpec(memory_space=pl.ANY)] * count,
        out_specs=[pl.BlockSpec(memory_space=pl.ANY)] * count,
        scratch_shapes=[
            pltpu.SemaphoreType.DMA((count, n)),
            pltpu.SemaphoreType.DMA((count, n)),
            pltpu.SemaphoreType.DMA((count,)),
        ],
        compiler_params=pltpu.CompilerParams(collective_id=collective_id, has_side_effects=True),
        cost_estimate=pl.CostEstimate(
            flops=0, bytes_accessed=int(cost_us * 3.0e6), transcendentals=0
        ),
    )(*arrays)


def pair_entry(n):
    me = lax.axis_index("kv")
    par = lax.rem(me, 2)
    idx = me // 2
    partner = me + 1 - 2 * par
    half = n // 2
    barrier = pltpu.get_barrier_semaphore()
    for t in range(half):
        peer = partner if t == half - 1 else 2 * lax.rem(idx + 1 + t, half) + par
        pl.semaphore_signal(
            barrier, inc=1, device_id={"kv": peer}, device_id_type=pl.DeviceIdType.MESH
        )
    pl.semaphore_wait(barrier, half)
    return idx, par, partner


def send(src, dst, send_sem, recv_sem, peer):
    copy = pltpu.make_async_remote_copy(
        src_ref=src,
        dst_ref=dst,
        send_sem=send_sem,
        recv_sem=recv_sem,
        device_id={"kv": peer},
        device_id_type=pl.DeviceIdType.MESH,
    )
    copy.start()
    return copy


def gather_kernel(n, src, dst, line_send, line_recv, pair_send, pair_recv, local_sem):
    idx, par, partner = pair_entry(n)
    me = lax.axis_index("kv")
    half = n // 2
    line = []
    for t in range(half - 1):
        peer = 2 * lax.rem(idx + 1 + t, half) + par
        line.append(send(src, dst.at[me], line_send.at[t], line_recv.at[t], peer))
    pair = [send(src, dst.at[me], pair_send.at[half - 1], pair_recv.at[half - 1], partner)]
    own = pltpu.make_async_copy(src, dst.at[me], local_sem)
    own.start()
    for t in range(half - 1):
        line[t].wait_recv()
        origin = 2 * lax.rem(idx - 1 - t + half, half) + par
        pair.append(
            send(dst.at[origin], dst.at[origin], pair_send.at[t], pair_recv.at[t], partner)
        )
    for copy in line:
        copy.wait_send()
    for copy in pair:
        copy.wait()
    own.wait()


def gather_queries(query, n, collective_id):
    half = n // 2
    return pl.pallas_call(
        functools.partial(gather_kernel, n),
        out_shape=jax.ShapeDtypeStruct((n,) + query.shape, query.dtype),
        in_specs=[pl.BlockSpec(memory_space=pl.ANY)],
        out_specs=pl.BlockSpec(memory_space=pl.ANY),
        scratch_shapes=[pltpu.SemaphoreType.DMA((half,))] * 4 + [pltpu.SemaphoreType.DMA],
        compiler_params=pltpu.CompilerParams(collective_id=collective_id, has_side_effects=True),
        cost_estimate=pl.CostEstimate(flops=0, bytes_accessed=200_000_000, transcendentals=0),
    )(query)


def reduce_kernel(
    n, value, residual, out, pair_buf, sum_buf, line_buf, line_send, line_recv, pair_send, pair_recv
):
    idx, par, partner = pair_entry(n)
    half = n // 2
    rows, width = out.shape
    step = 64
    pair = []
    line = []
    for t in range(half):
        first = (2 * lax.rem(idx + 1 + t, half) + 1 - par) * width
        strip = value.at[:, pl.ds(pl.multiple_of(first, width), width)]
        pair.append(send(strip, pair_buf.at[t], pair_send.at[t], pair_recv.at[t], partner))
    for t in range(half):
        peer = 2 * lax.rem(idx + 1 + t, half) + par
        columns = pl.ds(pl.multiple_of(peer * width, width), width)
        pair[t].wait_recv()

        @pl.loop(0, rows // step)
        def _(i):
            some = pl.ds(pl.multiple_of(i * step, step), step)
            both = value[some, columns].astype(jnp.float32) + pair_buf[t, some, :].astype(
                jnp.float32
            )
            if t == half - 1:
                out[some, :] = residual[some, :].astype(jnp.float32) + both
            else:
                sum_buf[t, some, :] = both.astype(jnp.bfloat16)

        if t < half - 1:
            line.append(
                send(sum_buf.at[t], line_buf.at[t], line_send.at[t], line_recv.at[t], peer)
            )
    for t in range(half - 1):
        line[t].wait_recv()

        @pl.loop(0, rows // step)
        def _(i):
            some = pl.ds(pl.multiple_of(i * step, step), step)
            out[some, :] += line_buf[t, some, :].astype(jnp.float32)

    for copy in pair + line:
        copy.wait_send()


def reduce_output(value, residual, n, collective_id):
    half = n // 2
    rows, width = residual.shape
    vmem = pl.BlockSpec(memory_space=pltpu.VMEM)
    return pl.pallas_call(
        functools.partial(reduce_kernel, n),
        out_shape=jax.ShapeDtypeStruct((rows, width), jnp.float32),
        in_specs=[vmem, vmem],
        out_specs=vmem,
        scratch_shapes=[pltpu.VMEM((half, rows, width), jnp.bfloat16)] * 3
        + [pltpu.SemaphoreType.DMA((half,))] * 4,
        compiler_params=pltpu.CompilerParams(
            collective_id=collective_id,
            has_side_effects=True,
            vmem_limit_bytes=24 * 1024 * 1024,
        ),
        cost_estimate=pl.CostEstimate(flops=0, bytes_accessed=200_000_000, transcendentals=0),
    )(value, residual)


def attention_kernel(
    groups, span, heads, slots, owner_ref, base_ref, len_ref, q_ref, cache_ref, acc_ref, stat_ref,
    s_scr, a_scr,
):
    scale = 1.0 / HD**0.5
    place = lax.broadcasted_iota(jnp.int32, (PAGE, span), 0)
    half = stat_ref.shape[2] // 2
    stat_ref[...] = jnp.zeros_like(stat_ref)
    for h in range(heads):
        tops = [jnp.full((1, span), FLOOR, jnp.float32) for _ in range(groups)]
        for s in range(slots):
            owner = owner_ref[s]
            q = q_ref[0, pl.ds(pl.multiple_of(owner * span, span), span), h * HD : (h + 1) * HD]
            st = lax.dot_general(
                cache_ref[s, 0, h], q, (((1,), (1,)), ((), ())), preferred_element_type=jnp.float32
            )
            st = jnp.where(place < len_ref[owner] - base_ref[s], st * scale, LOW)
            s_scr[s] = st
            col = jnp.max(st, axis=0, keepdims=True)
            tops = [jnp.maximum(t, jnp.where(owner == r, col, LOW)) for r, t in enumerate(tops)]
        sums = [jnp.zeros((1, span), jnp.float32) for _ in range(groups)]
        a_scr[...] = jnp.zeros_like(a_scr)
        for s in range(slots):
            owner = owner_ref[s]
            top = tops[0]
            for r in range(1, groups):
                top = jnp.where(owner == r, tops[r], top)
            p = jnp.exp(s_scr[s] - top).astype(jnp.bfloat16)
            part = jnp.sum(p.astype(jnp.float32), axis=0, keepdims=True)
            sums = [t + jnp.where(owner == r, part, 0.0) for r, t in enumerate(sums)]
            a_scr[owner] += lax.dot_general(
                cache_ref[s, 1, h], p, (((0,), (0,)), ((), ())), preferred_element_type=jnp.float32
            )
        for r in range(groups):
            acc_ref[0, r, h] = a_scr[r].astype(jnp.bfloat16)
            stat_ref[0, r, h : h + 1, :] = tops[r]
            stat_ref[0, r, half + h : half + h + 1, :] = sums[r]


def paged_attention(q_all, local_cache, owner_req, base, cached_len, groups, span, heads, half):
    n = q_all.shape[0]
    slots = local_cache.shape[0]
    rows, width = q_all.shape[1:]
    smem = pl.BlockSpec(memory_space=pltpu.SMEM)
    return pl.pallas_call(
        functools.partial(attention_kernel, groups, span, heads, slots),
        grid=(n,),
        out_shape=[
            jax.ShapeDtypeStruct((n, groups, heads, HD, span), jnp.bfloat16),
            jax.ShapeDtypeStruct((n, groups, 2 * half, span), jnp.float32),
        ],
        in_specs=[
            smem,
            smem,
            smem,
            pl.BlockSpec((1, rows, width), lambda j: (j, 0, 0)),
            pl.BlockSpec((slots, 2, heads, PAGE, HD), lambda j: (0, 0, j, 0, 0)),
        ],
        out_specs=[
            pl.BlockSpec((1, groups, heads, HD, span), lambda j: (j, 0, 0, 0, 0)),
            pl.BlockSpec((1, groups, 2 * half, span), lambda j: (j, 0, 0, 0)),
        ],
        scratch_shapes=[
            pltpu.VMEM((slots, PAGE, span), jnp.float32),
            pltpu.VMEM((groups, HD, span), jnp.float32),
        ],
        compiler_params=pltpu.CompilerParams(vmem_limit_bytes=32 * 1024 * 1024),
        cost_estimate=pl.CostEstimate(
            flops=4 * slots * HEADS * span * PAGE * HD,
            bytes_accessed=60_000_000,
            transcendentals=slots * HEADS * span * PAGE,
        ),
    )(owner_req, base, cached_len, q_all, local_cache)


def after(x, y):
    return lax.optimization_barrier((x, y))[0]


def per_device(
    hidden_in,
    ln_gains,
    qkv_weight,
    dense_weight,
    up_weight,
    down_weight,
    cache,
    cached_len,
    page_table,
):
    n_kv = lax.axis_size("kv")
    me_kv = lax.axis_index("kv")
    rows = hidden_in.shape[0]
    groups_here = cached_len.shape[0]
    span_rows = rows // groups_here
    width_loc = qkv_weight.shape[2]
    heads_loc = width_loc // HD
    half = max(4, heads_loc)
    scale = 1.0 / HD**0.5
    x = hidden_in.astype(jnp.float32)
    h1 = layer_norm(x, ln_gains[0]).astype(jnp.bfloat16)
    h2 = layer_norm(x, ln_gains[1]).astype(jnp.bfloat16)
    qkv_piece = lax.all_gather(qkv_weight, "req", axis=0, tiled=True)
    up_piece = lax.all_gather(after(up_weight, qkv_piece), "req", axis=0, tiled=True)
    count = qkv_piece.shape[0]
    qkv = jnp.dot(
        h1, qkv_piece.reshape(count, 3 * width_loc), preferred_element_type=jnp.float32
    )
    qkv = qkv.reshape(rows, 3, heads_loc, HD)
    offsets = jnp.arange(span_rows, dtype=jnp.int32)
    pos = (cached_len[:, None] + offsets[None, :]).reshape(rows).astype(jnp.float32)
    query = rotate(qkv[:, 0], pos).astype(jnp.bfloat16)
    key_new = rotate(qkv[:, 1], pos).astype(jnp.bfloat16)
    value_new = qkv[:, 2].astype(jnp.bfloat16)

    q_all = gather_queries(query.reshape(rows, width_loc), n_kv, 1)
    block = lambda ref, peer: ref.at[peer]
    local_cache = cache[0]
    slots_here = local_cache.shape[0]
    slot_ids = me_kv * slots_here + jnp.arange(slots_here, dtype=jnp.int32)
    match = (page_table[None, :, :] == slot_ids[:, None, None]).astype(jnp.int32)
    owner_req = jnp.sum(
        match * jnp.arange(groups_here, dtype=jnp.int32)[None, :, None], axis=(1, 2)
    )
    owner_page = jnp.sum(
        match * jnp.arange(page_table.shape[1], dtype=jnp.int32)[None, None, :], axis=(1, 2)
    )
    acc, stat = paged_attention(
        q_all,
        local_cache,
        owner_req,
        owner_page * PAGE,
        cached_len,
        groups_here,
        span_rows,
        heads_loc,
        half,
    )
    up_piece = after(up_piece, stat)
    dense_piece = lax.all_gather(after(dense_weight, up_piece), "req", axis=1, tiled=True)
    down_piece = lax.all_gather(after(down_weight, up_piece), "req", axis=1, tiled=True)
    acc_in, stat_in = exchange(
        [acc, stat], [block, block], [acc.shape[1:], stat.shape[1:]], n_kv, 2, 80
    )

    q_grp = query.reshape(groups_here, span_rows, heads_loc, HD)
    k_grp = key_new.reshape(groups_here, span_rows, heads_loc, HD)
    v_grp = value_new.reshape(groups_here, span_rows, heads_loc, HD)
    causal = (offsets[None, :] <= offsets[:, None])[None, None]
    s_new = jnp.einsum("gqhd,gkhd->ghqk", q_grp, k_grp, preferred_element_type=jnp.float32) * scale
    s_new = jnp.where(causal, s_new, LOW)
    top_new = jnp.max(s_new, axis=-1)
    p_new = jnp.where(causal, jnp.exp(s_new - top_new[..., None]), 0.0).astype(jnp.bfloat16)
    total_new = jnp.sum(p_new.astype(jnp.float32), axis=-1)
    accum_new = jnp.einsum("ghqk,gkhd->ghdq", p_new, v_grp, preferred_element_type=jnp.float32)

    tops = stat_in[:, :, :heads_loc, :]
    totals = stat_in[:, :, half : half + heads_loc, :]
    largest = jnp.maximum(jnp.max(tops, axis=0), top_new)
    factor = jnp.exp(tops - largest[None])
    fresh = jnp.exp(top_new - largest)
    denom = jnp.sum(totals * factor, axis=0) + total_new * fresh
    numer = jnp.sum(acc_in.astype(jnp.float32) * factor[:, :, :, None, :], axis=0)
    numer = numer + accum_new * fresh[:, :, None, :]
    att = (numer / denom[:, :, None, :]).astype(jnp.bfloat16)
    att = jnp.transpose(att, (0, 3, 1, 2)).reshape(rows, width_loc)

    up_acc = jnp.dot(h2, up_piece, preferred_element_type=jnp.float32)
    hidden = jax.nn.gelu(up_acc, approximate=False).astype(jnp.bfloat16)
    value = jnp.dot(att, dense_piece, preferred_element_type=jnp.float32) + jnp.dot(
        hidden, down_piece, preferred_element_type=jnp.float32
    )
    width_out = D // n_kv
    residual = lax.dynamic_slice_in_dim(hidden_in, me_kv * width_out, width_out, 1)
    return reduce_output(value.astype(jnp.bfloat16), residual, n_kv, 3)


def solution(mesh):
    placed = (
        P("req", None),
        P(),
        P("req", None, "kv"),
        P("kv", "req"),
        P("req", "kv"),
        P("kv", "req"),
        P("req", "kv", None, None, None, None),
        P("req"),
        P("req", None),
    )
    return jax.shard_map(
        per_device, mesh=mesh, in_specs=placed, out_specs=P("req", "kv"), check_vma=False
    )
```
